32 devices in a mesh: groups: 2 (over x), tok: 4 (over y, core), hid: 4 (over z).
Axes of the slice: x: 2, y: 2, z: 4, core: 2. Of those that a mesh axis runs over, the one named last changes fastest.
Arguments:
- tokens: bfloat16 [2048, 5376], P(('groups', 'tok'), 'hid'), parts along dimension 0, may hold values from -6 to 6
- w_query: bfloat16 [5376, 2048], P('tok', 'hid'), may hold values from -0.078125 to 0.078125
- key_weight: bfloat16 [5376, 1024], P('tok', 'hid'), may hold values from -0.078125 to 0.078125
- value_weight: bfloat16 [5376, 1024], P('tok', 'hid'), may hold values from -0.078125 to 0.078125
- w_out: bfloat16 [2048, 5376], P('tok', 'hid'), may hold values from -0.5 to 0.5
- query_norm_gain: float32 [128], replicated, may hold values from 0.5 to 2
- key_gain: float32 [128], replicated, may hold values from 0.5 to 2
- positions: int32 [2048], P('groups'), parts along dimension 0, may hold values from 0 to 131071, as said below
- grad_out: bfloat16 [2048, 5376], P(('groups', 'tok'), 'hid'), parts along dimension 0, may hold values from -6 to 6
Outputs:
- attn_out: bfloat16 [2048, 5376], P(('groups', 'tok'), 'hid'), parts along dimension 0
- grad_x: bfloat16 [2048, 5376], P(('groups', 'tok'), 'hid'), parts along dimension 0
- grad_wq: float32 [10752, 2048], P(('groups', 'tok'), 'hid'), parts along dimension 0
- key_weight_gradient: float32 [10752, 1024], P(('groups', 'tok'), 'hid'), parts along dimension 0
- value_weight_gradient: float32 [10752, 1024], P(('groups', 'tok'), 'hid'), parts along dimension 0
- grad_wo: float32 [4096, 5376], P(('groups', 'tok'), 'hid'), parts along dimension 0
The draws below stay inside these ranges and needn't reach their ends.
There are 2 independent parts, one for each index of `groups`. The reference program is written for one: setup_inputs(seed, part) draws one part's arguments, and reference() takes and returns one part's arrays. A program takes and returns all parts, laid end to end along the dimension named above; an argument that names none is the same for every part. Nothing has to cross between parts.
Inputs may be any that keep to these rules, and one draw needn't show every extreme that they name: positions[t] is token t's position in its document: it rises by one from token to token and is 0 where a document begins; the first document begins before the window and its last token in the window has position 131071; at least one document begins inside the window.
All inputs are finite; a program needn't handle non-finite values.
Results may differ from the reference program's by a relative error of at most 0.02.
Values may be sent and summed in bfloat16 or wider, within the bound.
A program may use at most 192 MiB of HBM per device.

```python
import math
import jax
import jax.numpy as jnp
from jax import lax

MODEL_WIDTH = 5376
QUERY_HEADS = 16
KEY_VALUE_HEADS = 8
HEAD_SIZE = 128
WINDOW = 1024
TOK_DEV = 256
WINDOW_TOKENS = 1024
N_TOK = 4


def draw_positions(key, part):
    start_key = jax.random.fold_in(key, 11)
    forced_key = jax.random.fold_in(key, 12)
    token_index = jnp.arange(WINDOW_TOKENS, dtype=jnp.int32)
    begins = jax.random.randint(start_key, (WINDOW_TOKENS,), 0, WINDOW, dtype=jnp.int32) == 0
    forced_at = jax.random.randint(forced_key, (), 1, WINDOW_TOKENS, dtype=jnp.int32)
    begins = (begins | (token_index == forced_at)) & (token_index > 0)
    latest = lax.cummax(jnp.where(begins, token_index, -1), axis=0)
    first_begin = jnp.min(jnp.where(begins, token_index, WINDOW_TOKENS))
    leading = 131072 - first_begin + token_index
    return jnp.where(latest < 0, leading, token_index - latest).astype(jnp.int32)


def steps_of(own_key, extent, pieces, low, top_value):
    level, own = 1.0, jax.random.fold_in(own_key, 6)
    for position, parts in pieces:
        draws = jnp.exp(jax.random.uniform(jax.random.fold_in(own, position), (parts,), jnp.float32, low / len(pieces), top_value / len(pieces)))
        level = level * jnp.repeat(draws, extent[position] // parts).reshape([-1 if axis == position else 1 for axis in range(len(extent))])
    return level


def normal_values(stream_key, shape, spread, bound, pieces=(), held_as=jnp.bfloat16):
    array = spread * jax.random.normal(stream_key, shape, jnp.float32)
    if pieces:
        array = array * steps_of(stream_key, shape, pieces, -0.22, 0.18)
    return jnp.clip(array, -bound, bound).astype(held_as)


def setup_inputs(seed: int = 0, part: int = 0) -> dict:
    key_list = jax.random.split(jax.random.key(seed), 10)
    part_splits = jax.random.split(jax.random.fold_in(key_list[9], part), 10)
    tokens = normal_values(part_splits[0], (WINDOW_TOKENS, MODEL_WIDTH), 1.0, 6.0, ((0, 4), (1, 4)))
    w_query = normal_values(key_list[1], (MODEL_WIDTH, QUERY_HEADS * HEAD_SIZE), MODEL_WIDTH ** -0.5, 0.078125, ((0, 4), (1, 4)))
    key_weight = normal_values(key_list[2], (MODEL_WIDTH, KEY_VALUE_HEADS * HEAD_SIZE), MODEL_WIDTH ** -0.5, 0.078125, ((0, 4), (1, 4)))
    value_weight = normal_values(key_list[3], (MODEL_WIDTH, KEY_VALUE_HEADS * HEAD_SIZE), MODEL_WIDTH ** -0.5, 0.078125, ((0, 4), (1, 4)))
    w_out = normal_values(key_list[4], (QUERY_HEADS * HEAD_SIZE, MODEL_WIDTH), HEAD_SIZE ** -0.5, 0.5, ((0, 4), (1, 4)))
    query_norm_gain = jnp.clip(jnp.exp(jax.random.uniform(key_list[5], (HEAD_SIZE,), jnp.float32, math.log(0.5), math.log(2.0))), 0.5, 2.0)
    key_gain = jnp.clip(jnp.exp(jax.random.uniform(key_list[6], (HEAD_SIZE,), jnp.float32, math.log(0.5), math.log(2.0))), 0.5, 2.0)
    positions = draw_positions(jax.random.fold_in(jax.random.fold_in(key_list[9], part), 71), part)
    grad_out = normal_values(part_splits[8], (WINDOW_TOKENS, MODEL_WIDTH), 1.0, 6.0, ((0, 4), (1, 4)))
    return dict(tokens=tokens, w_query=w_query, key_weight=key_weight, value_weight=value_weight, w_out=w_out, query_norm_gain=query_norm_gain, key_gain=key_gain, positions=positions, grad_out=grad_out)


attn_scale = 168.0 ** (-0.5)
rope_base = 10000.0
norm_eps = 1e-06

def cast_to_bfloat(values_in):
    return lax.optimization_barrier(values_in.astype(jnp.bfloat16))

def rotary_tables(token_pos):
    half_dim = HEAD_SIZE // 2
    freqs = rope_base ** (-jnp.arange(half_dim, dtype=jnp.float32) * 2.0 / HEAD_SIZE)
    angles = token_pos.astype(jnp.float32)[:, None] * freqs[None, :]
    return (jnp.cos(angles), jnp.sin(angles))

def prepare_inputs(raw_values, gain_vector, cosine_table, sine_table):
    scaled = raw_values * lax.rsqrt(lax.optimization_barrier(jnp.mean(raw_values * raw_values, -1, keepdims=True)) + norm_eps) * gain_vector
    half_dim = scaled.shape[-1] // 2
    first_half = scaled[..., :half_dim]
    second_half = scaled[..., half_dim:]
    cos_rows = cosine_table[:, None, :]
    sin_rows = sine_table[:, None, :]
    return jnp.concatenate([first_half * cos_rows - second_half * sin_rows, second_half * cos_rows + first_half * sin_rows], -1)

def probabilities_of(query_block, key_window, allowed):
    scores = jnp.einsum('tkgd,ukd->kgtu', query_block.astype(jnp.float32), key_window.astype(jnp.float32)) * attn_scale
    weights = jnp.where(allowed[None, None], jnp.exp(scores), 0.0)
    return weights / lax.optimization_barrier(jnp.sum(weights, -1, keepdims=True))

def block_sum(left_side, right_side):

    def advance(running, block_index):
        left_block = lax.dynamic_slice_in_dim(left_side, block_index * TOK_DEV, TOK_DEV, 0)
        right_block = lax.dynamic_slice_in_dim(right_side, block_index * TOK_DEV, TOK_DEV, 0)
        product = jnp.dot(left_block.T, right_block, preferred_element_type=jnp.float32)
        return (running + cast_to_bfloat(product).astype(jnp.float32), None)
    start_sum = jnp.zeros((left_side.shape[1], right_side.shape[1]), jnp.float32)
    total, _ = lax.scan(advance, start_sum, jnp.arange(N_TOK, dtype=jnp.int32))
    return total

def reference(tokens, w_query, key_weight, value_weight, w_out, query_norm_gain, key_gain, positions, grad_out):
    group_width = QUERY_HEADS // KEY_VALUE_HEADS
    reach = WINDOW // TOK_DEV
    span_rows = (reach + 1) * TOK_DEV
    cosine_table, sine_table = rotary_tables(positions)
    query_unnormed = jnp.dot(tokens, w_query, preferred_element_type=jnp.float32).reshape(WINDOW_TOKENS, QUERY_HEADS, HEAD_SIZE)
    key_unnormed = jnp.dot(tokens, key_weight, preferred_element_type=jnp.float32).reshape(WINDOW_TOKENS, KEY_VALUE_HEADS, HEAD_SIZE)
    value_rows = cast_to_bfloat(jnp.dot(tokens, value_weight, preferred_element_type=jnp.float32)).reshape(WINDOW_TOKENS, KEY_VALUE_HEADS, HEAD_SIZE)
    query_rows = cast_to_bfloat(prepare_inputs(query_unnormed, query_norm_gain, cosine_table, sine_table)).reshape(WINDOW_TOKENS, KEY_VALUE_HEADS, group_width, HEAD_SIZE)
    keys = cast_to_bfloat(prepare_inputs(key_unnormed, key_gain, cosine_table, sine_table))
    leading_part = reach * TOK_DEV
    keys_padded = jnp.pad(keys, ((leading_part, 0), (0, 0), (0, 0)))
    values_padded = jnp.pad(value_rows, ((leading_part, 0), (0, 0), (0, 0)))
    pos_padded = jnp.pad(positions, (leading_part, 0))

    def window_of(block_index):
        first_token = block_index * TOK_DEV
        query_block = lax.dynamic_slice_in_dim(query_rows, first_token, TOK_DEV, 0)
        key_window = lax.dynamic_slice_in_dim(keys_padded, first_token, span_rows, 0)
        value_window = lax.dynamic_slice_in_dim(values_padded, first_token, span_rows, 0)
        query_index = first_token + jnp.arange(TOK_DEV, dtype=jnp.int32)
        key_index = first_token - leading_part + jnp.arange(span_rows, dtype=jnp.int32)
        query_pos = lax.dynamic_slice_in_dim(positions, first_token, TOK_DEV, 0)
        key_pos = lax.dynamic_slice_in_dim(pos_padded, first_token, span_rows, 0)
        distance = query_index[:, None] - key_index[None, :]
        allowed = (key_index[None, :] >= 0) & (distance >= 0) & (distance < WINDOW) & (query_pos[:, None] - key_pos[None, :] == distance)
        return (query_block, key_window, value_window, allowed)

    def forward_block(block_index):
        query_block, key_window, value_window, allowed = window_of(block_index)
        probs_block = probabilities_of(query_block, key_window, allowed)
        rounded = cast_to_bfloat(probs_block).astype(jnp.float32)
        return jnp.einsum('kgtu,ukd->tkgd', rounded, value_window.astype(jnp.float32)).astype(jnp.bfloat16)
    attended = lax.map(forward_block, jnp.arange(N_TOK, dtype=jnp.int32)).reshape(WINDOW_TOKENS, QUERY_HEADS * HEAD_SIZE)
    attn_out = jnp.dot(attended, w_out, preferred_element_type=jnp.float32).astype(jnp.bfloat16)
    attended_gradient = cast_to_bfloat(jnp.dot(grad_out, w_out.T, preferred_element_type=jnp.float32))
    grad_wo = block_sum(attended, grad_out)
    heads_gradient = attended_gradient.reshape(WINDOW_TOKENS, KEY_VALUE_HEADS, group_width, HEAD_SIZE)

    def backward_block(running, block_index):
        key_pad_grad, value_pad_grad = running
        query_block, key_window, value_window, allowed = window_of(block_index)
        probs_block = probabilities_of(query_block, key_window, allowed)
        rounded = cast_to_bfloat(probs_block).astype(jnp.float32)
        first_token = block_index * TOK_DEV
        grad_block = lax.dynamic_slice_in_dim(heads_gradient, first_token, TOK_DEV, 0).astype(jnp.float32)
        grad_probs = jnp.einsum('tkgd,ukd->kgtu', grad_block, value_window.astype(jnp.float32))
        grad_scores = attn_scale * probs_block * (grad_probs - lax.optimization_barrier(jnp.sum(probs_block * grad_probs, -1, keepdims=True)))
        grad_scores = cast_to_bfloat(grad_scores).astype(jnp.float32)
        query_grad = jnp.einsum('kgtu,ukd->tkgd', grad_scores, key_window.astype(jnp.float32))
        key_grad = jnp.einsum('kgtu,tkgd->ukd', grad_scores, query_block.astype(jnp.float32))
        value_grad = jnp.einsum('kgtu,tkgd->ukd', rounded, grad_block)
        key_sum = lax.dynamic_slice_in_dim(key_pad_grad, first_token, span_rows, 0) + key_grad
        value_sum = lax.dynamic_slice_in_dim(value_pad_grad, first_token, span_rows, 0) + value_grad
        key_pad_grad = lax.dynamic_update_slice_in_dim(key_pad_grad, key_sum, first_token, 0)
        value_pad_grad = lax.dynamic_update_slice_in_dim(value_pad_grad, value_sum, first_token, 0)
        return ((key_pad_grad, value_pad_grad), query_grad)
    zero_padding = jnp.zeros((WINDOW_TOKENS + leading_part, KEY_VALUE_HEADS, HEAD_SIZE), jnp.float32)
    (key_pad_grad, value_pad_grad), query_grads = lax.scan(backward_block, (zero_padding, zero_padding), jnp.arange(N_TOK, dtype=jnp.int32))
    grad_queries = query_grads.reshape(WINDOW_TOKENS, QUERY_HEADS, HEAD_SIZE)
    keys_gradient = key_pad_grad[leading_part:]
    values_gradient = value_pad_grad[leading_part:]
    _, query_pull = jax.vjp(lambda raw_values: prepare_inputs(raw_values, query_norm_gain, cosine_table, sine_table), query_unnormed)
    _, key_pullback = jax.vjp(lambda raw_values: prepare_inputs(raw_values, key_gain, cosine_table, sine_table), key_unnormed)
    query_back = cast_to_bfloat(query_pull(grad_queries)[0]).reshape(WINDOW_TOKENS, QUERY_HEADS * HEAD_SIZE)
    key_backward = cast_to_bfloat(key_pullback(keys_gradient)[0]).reshape(WINDOW_TOKENS, KEY_VALUE_HEADS * HEAD_SIZE)
    value_backward = cast_to_bfloat(values_gradient).reshape(WINDOW_TOKENS, KEY_VALUE_HEADS * HEAD_SIZE)
    grad_sum = jnp.dot(query_back, w_query.T, preferred_element_type=jnp.float32)
    grad_sum = grad_sum + jnp.dot(key_backward, key_weight.T, preferred_element_type=jnp.float32)
    grad_sum = grad_sum + jnp.dot(value_backward, value_weight.T, preferred_element_type=jnp.float32)
    grad_x = grad_sum.astype(jnp.bfloat16)
    joined = jnp.concatenate([query_back, key_backward, value_backward], 1)
    inputs_gradient = block_sum(tokens, joined)
    grad_wq = inputs_gradient[:, :QUERY_HEADS * HEAD_SIZE]
    key_weight_gradient = inputs_gradient[:, QUERY_HEADS * HEAD_SIZE:QUERY_HEADS * HEAD_SIZE + KEY_VALUE_HEADS * HEAD_SIZE]
    value_weight_gradient = inputs_gradient[:, QUERY_HEADS * HEAD_SIZE + KEY_VALUE_HEADS * HEAD_SIZE:]
    return (attn_out, grad_x, grad_wq, key_weight_gradient, value_weight_gradient, grad_wo)
```

```python
import jax
import jax.numpy as jnp
from jax import lax
from jax.sharding import PartitionSpec as P

QUERY_HEADS = 16
KEY_VALUE_HEADS = 8
HEAD_SIZE = 128
WINDOW = 1024
TOK_DEV = 256


attn_scale = 168.0 ** (-0.5)
rope_base = 10000.0
norm_eps = 1e-06


def shifted(value, axis, steps):
    count = lax.axis_size(axis)
    first, last = (max(0, -steps), min(count, count - steps))
    return lax.ppermute(value, axis, [(source, source + steps) for source in range(first, last)])


def swapped(value, axis, bit):
    count = lax.axis_size(axis)
    return lax.ppermute(value, axis, [(source, source ^ bit) for source in range(count)])


def gather_swapped(value, axis):
    count = lax.axis_size(axis)
    held = {0: value}
    bit = count // 2
    while bit:
        for offset in list(held):
            held[offset ^ bit] = swapped(held[offset], axis, bit)
        bit //= 2
    return [held[offset] for offset in range(count)]


def scatter_product(left, right, axis):
    count = lax.axis_size(axis)
    index = lax.axis_index(axis)
    height = left.shape[1] // count
    blocks = left.reshape(left.shape[0], count // 2, 2, height)

    def part(core):
        picked = lax.dynamic_index_in_dim(blocks, core, 2, keepdims=False)
        picked = picked.reshape(left.shape[0], (count // 2) * height)
        return jnp.einsum("td,tc->dc", picked, right, preferred_element_type=jnp.float32).astype(
            jnp.bfloat16
        )

    core = index % 2
    sent = part(1 - core)
    arrived = swapped(sent, axis, 1)
    kept = part(core)
    total = kept.astype(jnp.float32) + arrived.astype(jnp.float32)
    bit, remaining = 2, count // 2
    while remaining > 1:
        mine = (index // bit) % 2
        total = total.astype(jnp.bfloat16).reshape(remaining // 2, 2, height, right.shape[1])
        sent = lax.dynamic_index_in_dim(total, 1 - mine, 1, keepdims=False)
        kept = lax.dynamic_index_in_dim(total, mine, 1, keepdims=False)
        arrived = swapped(sent, axis, bit)
        total = kept.astype(jnp.float32) + arrived.astype(jnp.float32)
        bit, remaining = bit * 2, remaining // 2
    return total.reshape(height, right.shape[1])


def rotary_tables(token_pos):
    half_dim = HEAD_SIZE // 2
    freqs = rope_base ** (-jnp.arange(half_dim, dtype=jnp.float32) * 2.0 / HEAD_SIZE)
    angles = token_pos.astype(jnp.float32)[:, None] * freqs[None, :]
    return (jnp.cos(angles), jnp.sin(angles))


def prepare_inputs(raw_values, gain_vector, cosine_table, sine_table):
    scaled = (
        raw_values
        * lax.rsqrt(jnp.mean(raw_values * raw_values, -1, keepdims=True) + norm_eps)
        * gain_vector
    )
    half_dim = scaled.shape[-1] // 2
    first_half = scaled[..., :half_dim]
    second_half = scaled[..., half_dim:]
    cos_rows = cosine_table[:, None, :]
    sin_rows = sine_table[:, None, :]
    return jnp.concatenate(
        [
            first_half * cos_rows - second_half * sin_rows,
            second_half * cos_rows + first_half * sin_rows,
        ],
        -1,
    )


def local(
    tokens, w_query, key_weight, value_weight, w_out, query_norm_gain, key_gain, positions, grad_out
):
    hidden_count = lax.axis_size("hid")
    block_index = lax.axis_index("tok")
    query_heads = QUERY_HEADS // hidden_count
    key_value_heads = KEY_VALUE_HEADS // hidden_count
    group_width = QUERY_HEADS // KEY_VALUE_HEADS
    reach = min(WINDOW // TOK_DEV, lax.axis_size("tok") - 1)
    span_rows = (reach + 1) * TOK_DEV
    leading_part = reach * TOK_DEV
    first_token = block_index * TOK_DEV
    query_cols = query_heads * HEAD_SIZE
    kv_cols = key_value_heads * HEAD_SIZE
    full_rows = lax.all_gather(tokens, "hid", axis=1, tiled=True)
    query_pieces = gather_swapped(w_query, "tok")
    kv_pieces = gather_swapped(jnp.concatenate([key_weight, value_weight], 1), "tok")
    full_wo = lax.all_gather(w_out, "tok", axis=0, tiled=True)
    height = w_query.shape[0]

    def project(pieces):
        total = 0.0
        for offset, piece in enumerate(pieces):
            start = (block_index ^ offset) * height
            columns = lax.dynamic_slice_in_dim(full_rows, start, height, 1)
            total = total + jnp.dot(columns, piece, preferred_element_type=jnp.float32)
        return total

    kv_unnormed = project(kv_pieces)
    query_unnormed = project(query_pieces)
    key_unnormed = kv_unnormed[:, :kv_cols]
    value_raw = kv_unnormed[:, kv_cols:]
    partial_heads = jnp.einsum("td,hd->th", grad_out, full_wo, preferred_element_type=jnp.float32)
    attended_gradient = lax.psum_scatter(
        partial_heads.astype(jnp.bfloat16), "hid", scatter_dimension=1, tiled=True
    )
    values_local = value_raw.astype(jnp.bfloat16)
    token_pos = lax.dynamic_slice_in_dim(positions, first_token, TOK_DEV, 0)
    cosine_table, sine_table = rotary_tables(token_pos)
    query_heads_raw = query_unnormed.reshape(TOK_DEV, query_heads, HEAD_SIZE)
    key_heads_raw = key_unnormed.reshape(TOK_DEV, key_value_heads, HEAD_SIZE)
    query_rows = (
        prepare_inputs(query_heads_raw, query_norm_gain, cosine_table, sine_table)
        .astype(jnp.bfloat16)
        .reshape(TOK_DEV, key_value_heads, group_width, HEAD_SIZE)
    )
    keys_local = prepare_inputs(key_heads_raw, key_gain, cosine_table, sine_table).astype(
        jnp.bfloat16
    )
    key_value = jnp.concatenate([keys_local.reshape(TOK_DEV, kv_cols), values_local], 1)
    blocks = [shifted(key_value, "tok", steps) for steps in range(reach, 0, -1)] + [key_value]
    window = jnp.concatenate(blocks, 0)
    key_window = window[:, :kv_cols].reshape(span_rows, key_value_heads, HEAD_SIZE)
    value_window = window[:, kv_cols:].reshape(span_rows, key_value_heads, HEAD_SIZE)
    query_index = first_token + jnp.arange(TOK_DEV, dtype=jnp.int32)
    key_index = first_token - leading_part + jnp.arange(span_rows, dtype=jnp.int32)
    padded_pos = jnp.pad(positions, (leading_part, 0))
    key_pos = lax.dynamic_slice_in_dim(padded_pos, first_token, span_rows, 0)
    distance = query_index[:, None] - key_index[None, :]
    allowed = (
        (key_index[None, :] >= 0)
        & (distance >= 0)
        & (distance < WINDOW)
        & (token_pos[:, None] - key_pos[None, :] == distance)
    )
    scores = (
        jnp.einsum("tkgd,ukd->kgtu", query_rows, key_window, preferred_element_type=jnp.float32)
        * attn_scale
    )
    weights = jnp.where(allowed[None, None], jnp.exp(scores), 0.0)
    probabilities = weights / jnp.sum(weights, -1, keepdims=True)
    rounded = probabilities.astype(jnp.bfloat16)
    attended = jnp.einsum(
        "kgtu,ukd->tkgd", rounded, value_window, preferred_element_type=jnp.float32
    )
    attended = attended.astype(jnp.bfloat16).reshape(TOK_DEV, query_cols)
    all_heads = lax.all_gather(attended, "hid", axis=1, tiled=True)
    output = jnp.dot(all_heads, full_wo, preferred_element_type=jnp.float32)
    attn_out = output.astype(jnp.bfloat16)
    grad_wo = scatter_product(all_heads, grad_out, "tok")
    attended_gradient = attended_gradient.reshape(TOK_DEV, key_value_heads, group_width, HEAD_SIZE)
    grad_probs = jnp.einsum(
        "tkgd,ukd->kgtu", attended_gradient, value_window, preferred_element_type=jnp.float32
    )
    grad_scores = (
        attn_scale
        * probabilities
        * (grad_probs - jnp.sum(probabilities * grad_probs, -1, keepdims=True))
    )
    grad_scores = grad_scores.astype(jnp.bfloat16)
    grad_queries = jnp.einsum(
        "kgtu,ukd->tkgd", grad_scores, key_window, preferred_element_type=jnp.float32
    )
    keys_gradient = jnp.einsum(
        "kgtu,tkgd->ukd", grad_scores, query_rows, preferred_element_type=jnp.float32
    )
    values_gradient = jnp.einsum(
        "kgtu,tkgd->ukd", rounded, attended_gradient, preferred_element_type=jnp.float32
    )
    grad_window = jnp.concatenate(
        [keys_gradient.reshape(span_rows, kv_cols), values_gradient.reshape(span_rows, kv_cols)], 1
    )
    grad_kv = grad_window[leading_part:]
    for steps in range(reach, 0, -1):
        start = (reach - steps) * TOK_DEV
        block = grad_window[start : start + TOK_DEV].astype(jnp.bfloat16)
        grad_kv = grad_kv + shifted(block, "tok", -steps).astype(jnp.float32)
    _, query_pull = jax.vjp(
        lambda raw_values: prepare_inputs(raw_values, query_norm_gain, cosine_table, sine_table),
        query_heads_raw,
    )
    _, key_pullback = jax.vjp(
        lambda raw_values: prepare_inputs(raw_values, key_gain, cosine_table, sine_table),
        key_heads_raw,
    )
    query_back = (
        query_pull(grad_queries.reshape(TOK_DEV, query_heads, HEAD_SIZE))[0]
        .astype(jnp.bfloat16)
        .reshape(TOK_DEV, query_cols)
    )
    key_backward = (
        key_pullback(grad_kv[:, :kv_cols].reshape(TOK_DEV, key_value_heads, HEAD_SIZE))[0]
        .astype(jnp.bfloat16)
        .reshape(TOK_DEV, kv_cols)
    )
    value_backward = grad_kv[:, kv_cols:].astype(jnp.bfloat16)
    kv_back = jnp.concatenate([key_backward, value_backward], 1)
    block_rows = jnp.zeros((TOK_DEV, full_rows.shape[1]), jnp.bfloat16)
    for offset in range(len(query_pieces)):
        product = jnp.einsum(
            "tc,dc->td", query_back, query_pieces[offset], preferred_element_type=jnp.float32
        ) + jnp.einsum("tc,dc->td", kv_back, kv_pieces[offset], preferred_element_type=jnp.float32)
        start = (block_index ^ offset) * height
        block_rows = lax.dynamic_update_slice_in_dim(
            block_rows, product.astype(jnp.bfloat16), start, 1
        )
    grad_x = lax.psum_scatter(block_rows, "hid", scatter_dimension=1, tiled=True)
    grad_wq = scatter_product(full_rows, query_back, "tok")
    grad_wkv = scatter_product(full_rows, kv_back, "tok")
    key_weight_gradient = grad_wkv[:, :kv_cols]
    value_weight_gradient = grad_wkv[:, kv_cols:]
    return (attn_out, grad_x, grad_wq, key_weight_gradient, value_weight_gradient, grad_wo)


def solution(mesh):
    return jax.shard_map(
        local,
        mesh=mesh,
        in_specs=(
            P(("groups", "tok"), "hid"),
            P("tok", "hid"),
            P("tok", "hid"),
            P("tok", "hid"),
            P("tok", "hid"),
            P(),
            P(),
            P("groups"),
            P(("groups", "tok"), "hid"),
        ),
        out_specs=(
            P(("groups", "tok"), "hid"),
            P(("groups", "tok"), "hid"),
            P(("groups", "tok"), "hid"),
            P(("groups", "tok"), "hid"),
            P(("groups", "tok"), "hid"),
            P(("groups", "tok"), "hid"),
        ),
        check_vma=False,
    )
```

```python
import jax
import jax.numpy as jnp
from jax import lax
from jax.sharding import PartitionSpec as P

QUERY_HEADS = 16
KEY_VALUE_HEADS = 8
HEAD_SIZE = 128
WINDOW = 1024
TOK_DEV = 256


attn_scale = 168.0 ** (-0.5)
rope_base = 10000.0
norm_eps = 1e-06


def shifted(value, axis, steps):
    count = lax.axis_size(axis)
    first, last = (max(0, -steps), min(count, count - steps))
    return lax.ppermute(value, axis, [(source, source + steps) for source in range(first, last)])


def swapped(value, axis, bit):
    count = lax.axis_size(axis)
    return lax.ppermute(value, axis, [(source, source ^ bit) for source in range(count)])


def gather_swapped(value, axis):
    count = lax.axis_size(axis)
    held = {0: value}
    bit = count // 2
    while bit:
        for offset in list(held):
            held[offset ^ bit] = swapped(held[offset], axis, bit)
        bit //= 2
    return [held[offset] for offset in range(count)]


def begin_scatter(left, right, axis):
    count = lax.axis_size(axis)
    index = lax.axis_index(axis)
    height = left.shape[1] // count

    def product(offset):
        picked = lax.dynamic_slice_in_dim(left, (index ^ offset) * height, height, 1)
        return jnp.einsum("td,tc->dc", picked, right, preferred_element_type=jnp.float32)

    totals = {}
    for offset in range(count - 2, -1, -2):
        arrived = swapped(product(offset ^ 1).astype(jnp.bfloat16), axis, 1)
        totals[offset] = product(offset) + arrived.astype(jnp.float32)
        if offset:
            totals[offset] = totals[offset].astype(jnp.bfloat16)
    return totals


def finish_scatter(totals, axis):
    count = lax.axis_size(axis)
    totals = dict(totals)
    bit = 2
    while bit < count:
        for offset in range(count - bit, 0, -2 * bit):
            arrived = swapped(totals[offset], axis, bit).astype(jnp.float32)
            kept = offset ^ bit
            total = totals[kept].astype(jnp.float32) + arrived
            totals[kept] = total.astype(jnp.bfloat16) if kept else total
        bit *= 2
    return totals[0]


def ordered(value, *groups):
    sent = [{key: total for key, total in group.items() if key} for group in groups]
    value, sent = lax.optimization_barrier((value, sent))
    return value, [{**group, **part} for group, part in zip(groups, sent)]


def rotary_tables(token_pos):
    half_dim = HEAD_SIZE // 2
    freqs = rope_base ** (-jnp.arange(half_dim, dtype=jnp.float32) * 2.0 / HEAD_SIZE)
    angles = token_pos.astype(jnp.float32)[:, None] * freqs[None, :]
    return (jnp.cos(angles), jnp.sin(angles))


def prepare_inputs(raw_values, gain_vector, cosine_table, sine_table):
    scaled = (
        raw_values
        * lax.rsqrt(jnp.mean(raw_values * raw_values, -1, keepdims=True) + norm_eps)
        * gain_vector
    )
    half_dim = scaled.shape[-1] // 2
    first_half = scaled[..., :half_dim]
    second_half = scaled[..., half_dim:]
    cos_rows = cosine_table[:, None, :]
    sin_rows = sine_table[:, None, :]
    return jnp.concatenate(
        [
            first_half * cos_rows - second_half * sin_rows,
            second_half * cos_rows + first_half * sin_rows,
        ],
        -1,
    )


def local(
    tokens, w_query, key_weight, value_weight, w_out, query_norm_gain, key_gain, positions, grad_out
):
    hidden_count = lax.axis_size("hid")
    block_index = lax.axis_index("tok")
    query_heads = QUERY_HEADS // hidden_count
    key_value_heads = KEY_VALUE_HEADS // hidden_count
    group_width = QUERY_HEADS // KEY_VALUE_HEADS
    reach = min(WINDOW // TOK_DEV, lax.axis_size("tok") - 1)
    span_rows = (reach + 1) * TOK_DEV
    leading_part = reach * TOK_DEV
    first_token = block_index * TOK_DEV
    query_cols = query_heads * HEAD_SIZE
    kv_cols = key_value_heads * HEAD_SIZE
    full_rows = lax.all_gather(tokens, "hid", axis=1, tiled=True)
    query_pieces = gather_swapped(w_query, "tok")
    kv_pieces = gather_swapped(jnp.concatenate([key_weight, value_weight], 1), "tok")
    full_wo = lax.all_gather(w_out, "tok", axis=0, tiled=True)
    height = w_query.shape[0]

    def project(pieces):
        total = 0.0
        for offset, piece in enumerate(pieces):
            start = (block_index ^ offset) * height
            columns = lax.dynamic_slice_in_dim(full_rows, start, height, 1)
            total = total + jnp.dot(columns, piece, preferred_element_type=jnp.float32)
        return total

    kv_unnormed = project(kv_pieces)
    query_unnormed = project(query_pieces)
    key_unnormed = kv_unnormed[:, :kv_cols]
    value_raw = kv_unnormed[:, kv_cols:]
    partial_heads = jnp.einsum("td,hd->th", grad_out, full_wo, preferred_element_type=jnp.float32)
    attended_gradient = lax.psum_scatter(
        partial_heads.astype(jnp.bfloat16), "hid", scatter_dimension=1, tiled=True
    )
    values_local = value_raw.astype(jnp.bfloat16)
    token_pos = lax.dynamic_slice_in_dim(positions, first_token, TOK_DEV, 0)
    cosine_table, sine_table = rotary_tables(token_pos)
    query_heads_raw = query_unnormed.reshape(TOK_DEV, query_heads, HEAD_SIZE)
    key_heads_raw = key_unnormed.reshape(TOK_DEV, key_value_heads, HEAD_SIZE)
    query_rows = (
        prepare_inputs(query_heads_raw, query_norm_gain, cosine_table, sine_table)
        .astype(jnp.bfloat16)
        .reshape(TOK_DEV, key_value_heads, group_width, HEAD_SIZE)
    )
    keys_local = prepare_inputs(key_heads_raw, key_gain, cosine_table, sine_table).astype(
        jnp.bfloat16
    )
    key_value = jnp.concatenate([keys_local.reshape(TOK_DEV, kv_cols), values_local], 1)
    blocks = [shifted(key_value, "tok", steps) for steps in range(reach, 0, -1)] + [key_value]
    window = jnp.concatenate(blocks, 0)
    key_window = window[:, :kv_cols].reshape(span_rows, key_value_heads, HEAD_SIZE)
    value_window = window[:, kv_cols:].reshape(span_rows, key_value_heads, HEAD_SIZE)
    query_index = first_token + jnp.arange(TOK_DEV, dtype=jnp.int32)
    key_index = first_token - leading_part + jnp.arange(span_rows, dtype=jnp.int32)
    padded_pos = jnp.pad(positions, (leading_part, 0))
    key_pos = lax.dynamic_slice_in_dim(padded_pos, first_token, span_rows, 0)
    distance = query_index[:, None] - key_index[None, :]
    allowed = (
        (key_index[None, :] >= 0)
        & (distance >= 0)
        & (distance < WINDOW)
        & (token_pos[:, None] - key_pos[None, :] == distance)
    )
    scores = (
        jnp.einsum("tkgd,ukd->kgtu", query_rows, key_window, preferred_element_type=jnp.float32)
        * attn_scale
    )
    weights = jnp.where(allowed[None, None], jnp.exp(scores), 0.0)
    probabilities = weights / jnp.sum(weights, -1, keepdims=True)
    rounded = probabilities.astype(jnp.bfloat16)
    attended = jnp.einsum(
        "kgtu,ukd->tkgd", rounded, value_window, preferred_element_type=jnp.float32
    )
    attended = attended.astype(jnp.bfloat16).reshape(TOK_DEV, query_cols)
    attended, attended_gradient = lax.optimization_barrier((attended, attended_gradient))
    all_heads = lax.all_gather(attended, "hid", axis=1, tiled=True)
    output = jnp.dot(all_heads, full_wo, preferred_element_type=jnp.float32)
    attn_out = output.astype(jnp.bfloat16)
    attended_gradient = attended_gradient.reshape(TOK_DEV, key_value_heads, group_width, HEAD_SIZE)
    grad_probs = jnp.einsum(
        "tkgd,ukd->kgtu", attended_gradient, value_window, preferred_element_type=jnp.float32
    )
    grad_scores = (
        attn_scale
        * probabilities
        * (grad_probs - jnp.sum(probabilities * grad_probs, -1, keepdims=True))
    )
    grad_scores = grad_scores.astype(jnp.bfloat16)
    grad_queries = jnp.einsum(
        "kgtu,ukd->tkgd", grad_scores, key_window, preferred_element_type=jnp.float32
    )
    keys_gradient = jnp.einsum(
        "kgtu,tkgd->ukd", grad_scores, query_rows, preferred_element_type=jnp.float32
    )
    values_gradient = jnp.einsum(
        "kgtu,tkgd->ukd", rounded, attended_gradient, preferred_element_type=jnp.float32
    )
    grad_window = jnp.concatenate(
        [keys_gradient.reshape(span_rows, kv_cols), values_gradient.reshape(span_rows, kv_cols)], 1
    )
    grad_kv = grad_window[leading_part:]
    for steps in range(reach, 0, -1):
        start = (reach - steps) * TOK_DEV
        block = grad_window[start : start + TOK_DEV].astype(jnp.bfloat16)
        grad_kv = grad_kv + shifted(block, "tok", -steps).astype(jnp.float32)
    _, query_pull = jax.vjp(
        lambda raw_values: prepare_inputs(raw_values, query_norm_gain, cosine_table, sine_table),
        query_heads_raw,
    )
    _, key_pullback = jax.vjp(
        lambda raw_values: prepare_inputs(raw_values, key_gain, cosine_table, sine_table),
        key_heads_raw,
    )
    query_back = (
        query_pull(grad_queries.reshape(TOK_DEV, query_heads, HEAD_SIZE))[0]
        .astype(jnp.bfloat16)
        .reshape(TOK_DEV, query_cols)
    )
    key_backward = (
        key_pullback(grad_kv[:, :kv_cols].reshape(TOK_DEV, key_value_heads, HEAD_SIZE))[0]
        .astype(jnp.bfloat16)
        .reshape(TOK_DEV, kv_cols)
    )
    value_backward = grad_kv[:, kv_cols:].astype(jnp.bfloat16)
    kv_back = jnp.concatenate([key_backward, value_backward], 1)
    query_sums = begin_scatter(full_rows, query_back, "tok")
    out_sums = begin_scatter(all_heads, grad_out, "tok")
    kv_back, (query_sums, out_sums) = ordered(kv_back, query_sums, out_sums)
    block_rows = jnp.zeros((TOK_DEV, full_rows.shape[1]), jnp.bfloat16)
    for offset in range(len(query_pieces)):
        product = jnp.einsum(
            "tc,dc->td", query_back, query_pieces[offset], preferred_element_type=jnp.float32
        ) + jnp.einsum("tc,dc->td", kv_back, kv_pieces[offset], preferred_element_type=jnp.float32)
        start = (block_index ^ offset) * height
        block_rows = lax.dynamic_update_slice_in_dim(
            block_rows, product.astype(jnp.bfloat16), start, 1
        )
    grad_x = lax.psum_scatter(block_rows, "hid", scatter_dimension=1, tiled=True)
    kv_sums = begin_scatter(full_rows, kv_back, "tok")
    grad_wq = finish_scatter(query_sums, "tok")
    grad_wo = finish_scatter(out_sums, "tok")
    grad_wkv = finish_scatter(kv_sums, "tok")
    key_weight_gradient = grad_wkv[:, :kv_cols]
    value_weight_gradient = grad_wkv[:, kv_cols:]
    return (attn_out, grad_x, grad_wq, key_weight_gradient, value_weight_gradient, grad_wo)


def solution(mesh):
    return jax.shard_map(
        local,
        mesh=mesh,
        in_specs=(
            P(("groups", "tok"), "hid"),
            P("tok", "hid"),
            P("tok", "hid"),
            P("tok", "hid"),
            P("tok", "hid"),
            P(),
            P(),
            P("groups"),
            P(("groups", "tok"), "hid"),
        ),
        out_specs=(
            P(("groups", "tok"), "hid"),
            P(("groups", "tok"), "hid"),
            P(("groups", "tok"), "hid"),
            P(("groups", "tok"), "hid"),
            P(("groups", "tok"), "hid"),
            P(("groups", "tok"), "hid"),
        ),
        check_vma=False,
    )
```

```python
import jax
import jax.numpy as jnp
from jax import lax
from jax.sharding import PartitionSpec as P

QUERY_HEADS = 16
KEY_VALUE_HEADS = 8
HEAD_SIZE = 128
WINDOW = 1024
TOK_DEV = 256


attn_scale = 168.0 ** (-0.5)
rope_base = 10000.0
norm_eps = 1e-06


def shifted(value, axis, steps):
    count = lax.axis_size(axis)
    first, last = (max(0, -steps), min(count, count - steps))
    return lax.ppermute(value, axis, [(source, source + steps) for source in range(first, last)])


def swapped(value, axis, bit):
    count = lax.axis_size(axis)
    return lax.ppermute(value, axis, [(source, source ^ bit) for source in range(count)])


def gather_swapped(value, axis):
    count = lax.axis_size(axis)
    held = {0: value}
    bit = count // 2
    while bit:
        for offset in list(held):
            held[offset ^ bit] = swapped(held[offset], axis, bit)
        bit //= 2
    return [held[offset] for offset in range(count)]


def begin_scatter(left, right, axis):
    count = lax.axis_size(axis)
    index = lax.axis_index(axis)
    height = left.shape[1] // count

    def product(offset):
        picked = lax.dynamic_slice_in_dim(left, (index ^ offset) * height, height, 1)
        return jnp.einsum("td,tc->dc", picked, right, preferred_element_type=jnp.float32)

    totals = {}
    for offset in range(count - 2, -1, -2):
        arrived = swapped(product(offset ^ 1).astype(jnp.bfloat16), axis, 1)
        totals[offset] = product(offset) + arrived.astype(jnp.float32)
        if offset:
            totals[offset] = totals[offset].astype(jnp.bfloat16)
    return totals


def exchange_far(totals, axis):
    count = lax.axis_size(axis)
    totals = dict(totals)
    bit = 2
    while bit < count:
        for offset in range(count - bit, 0, -2 * bit):
            arrived = swapped(totals[offset], axis, bit)
            kept = offset ^ bit
            if kept == 0 and 2 * bit == count:
                return totals[0], arrived
            total = totals[kept].astype(jnp.float32) + arrived.astype(jnp.float32)
            totals[kept] = total.astype(jnp.bfloat16) if kept else total
        bit *= 2
    return totals[0], jnp.zeros_like(totals[0], jnp.bfloat16)


def finish(pair):
    return pair[0] + pair[1].astype(jnp.float32)


def ordered(value, *groups):
    sent = [{key: total for key, total in group.items() if key} for group in groups]
    value, sent = lax.optimization_barrier((value, sent))
    return value, [{**group, **part} for group, part in zip(groups, sent)]


def rotary_tables(token_pos):
    half_dim = HEAD_SIZE // 2
    freqs = rope_base ** (-jnp.arange(half_dim, dtype=jnp.float32) * 2.0 / HEAD_SIZE)
    angles = token_pos.astype(jnp.float32)[:, None] * freqs[None, :]
    return (jnp.cos(angles), jnp.sin(angles))


def prepare_inputs(raw_values, gain_vector, cosine_table, sine_table):
    scaled = (
        raw_values
        * lax.rsqrt(jnp.mean(raw_values * raw_values, -1, keepdims=True) + norm_eps)
        * gain_vector
    )
    half_dim = scaled.shape[-1] // 2
    first_half = scaled[..., :half_dim]
    second_half = scaled[..., half_dim:]
    cos_rows = cosine_table[:, None, :]
    sin_rows = sine_table[:, None, :]
    return jnp.concatenate(
        [
            first_half * cos_rows - second_half * sin_rows,
            second_half * cos_rows + first_half * sin_rows,
        ],
        -1,
    )


def local(
    tokens, w_query, key_weight, value_weight, w_out, query_norm_gain, key_gain, positions, grad_out
):
    hidden_count = lax.axis_size("hid")
    block_index = lax.axis_index("tok")
    query_heads = QUERY_HEADS // hidden_count
    key_value_heads = KEY_VALUE_HEADS // hidden_count
    group_width = QUERY_HEADS // KEY_VALUE_HEADS
    reach = min(WINDOW // TOK_DEV, lax.axis_size("tok") - 1)
    span_rows = (reach + 1) * TOK_DEV
    leading_part = reach * TOK_DEV
    first_token = block_index * TOK_DEV
    query_cols = query_heads * HEAD_SIZE
    kv_cols = key_value_heads * HEAD_SIZE
    full_rows = lax.all_gather(tokens, "hid", axis=1, tiled=True)
    query_pieces = gather_swapped(w_query, "tok")
    kv_pieces = gather_swapped(jnp.concatenate([key_weight, value_weight], 1), "tok")
    full_wo = lax.all_gather(w_out, "tok", axis=0, tiled=True)
    height = w_query.shape[0]

    def project(pieces):
        total = 0.0
        for offset, piece in enumerate(pieces):
            start = (block_index ^ offset) * height
            columns = lax.dynamic_slice_in_dim(full_rows, start, height, 1)
            total = total + jnp.dot(columns, piece, preferred_element_type=jnp.float32)
        return total

    kv_unnormed = project(kv_pieces)
    query_unnormed = project(query_pieces)
    key_unnormed = kv_unnormed[:, :kv_cols]
    value_raw = kv_unnormed[:, kv_cols:]
    partial_heads = jnp.einsum("td,hd->th", grad_out, full_wo, preferred_element_type=jnp.float32)
    partial_heads = partial_heads.astype(jnp.bfloat16)
    attended_gradient = lax.psum_scatter(partial_heads, "hid", scatter_dimension=1, tiled=True)
    values_local = value_raw.astype(jnp.bfloat16)
    token_pos = lax.dynamic_slice_in_dim(positions, first_token, TOK_DEV, 0)
    cosine_table, sine_table = rotary_tables(token_pos)
    query_heads_raw = query_unnormed.reshape(TOK_DEV, query_heads, HEAD_SIZE)
    key_heads_raw = key_unnormed.reshape(TOK_DEV, key_value_heads, HEAD_SIZE)
    query_rows = (
        prepare_inputs(query_heads_raw, query_norm_gain, cosine_table, sine_table)
        .astype(jnp.bfloat16)
        .reshape(TOK_DEV, key_value_heads, group_width, HEAD_SIZE)
    )
    keys_local = prepare_inputs(key_heads_raw, key_gain, cosine_table, sine_table).astype(
        jnp.bfloat16
    )
    key_value = jnp.concatenate([keys_local.reshape(TOK_DEV, kv_cols), values_local], 1)
    blocks = [shifted(key_value, "tok", steps) for steps in range(reach, 0, -1)] + [key_value]
    window = jnp.concatenate(blocks, 0)
    key_window = window[:, :kv_cols].reshape(span_rows, key_value_heads, HEAD_SIZE)
    value_window = window[:, kv_cols:].reshape(span_rows, key_value_heads, HEAD_SIZE)
    query_index = first_token + jnp.arange(TOK_DEV, dtype=jnp.int32)
    key_index = first_token - leading_part + jnp.arange(span_rows, dtype=jnp.int32)
    padded_pos = jnp.pad(positions, (leading_part, 0))
    key_pos = lax.dynamic_slice_in_dim(padded_pos, first_token, span_rows, 0)
    distance = query_index[:, None] - key_index[None, :]
    allowed = (
        (key_index[None, :] >= 0)
        & (distance >= 0)
        & (distance < WINDOW)
        & (token_pos[:, None] - key_pos[None, :] == distance)
    )
    scores = (
        jnp.einsum("tkgd,ukd->kgtu", query_rows, key_window, preferred_element_type=jnp.float32)
        * attn_scale
    )
    weights = jnp.where(allowed[None, None], jnp.exp(scores), 0.0)
    probabilities = weights / jnp.sum(weights, -1, keepdims=True)
    rounded = probabilities.astype(jnp.bfloat16)
    attended = jnp.einsum(
        "kgtu,ukd->tkgd", rounded, value_window, preferred_element_type=jnp.float32
    )
    attended = attended.astype(jnp.bfloat16).reshape(TOK_DEV, query_cols)
    attended, attended_gradient = lax.optimization_barrier((attended, attended_gradient))
    all_heads = lax.all_gather(attended, "hid", axis=1, tiled=True)
    output = jnp.dot(all_heads, full_wo, preferred_element_type=jnp.float32)
    attn_out = output.astype(jnp.bfloat16)
    attended_gradient = attended_gradient.reshape(TOK_DEV, key_value_heads, group_width, HEAD_SIZE)
    grad_probs = jnp.einsum(
        "tkgd,ukd->kgtu", attended_gradient, value_window, preferred_element_type=jnp.float32
    )
    grad_scores = (
        attn_scale
        * probabilities
        * (grad_probs - jnp.sum(probabilities * grad_probs, -1, keepdims=True))
    )
    grad_scores = grad_scores.astype(jnp.bfloat16)
    grad_queries = jnp.einsum(
        "kgtu,ukd->tkgd", grad_scores, key_window, preferred_element_type=jnp.float32
    )
    keys_gradient = jnp.einsum(
        "kgtu,tkgd->ukd", grad_scores, query_rows, preferred_element_type=jnp.float32
    )
    values_gradient = jnp.einsum(
        "kgtu,tkgd->ukd", rounded, attended_gradient, preferred_element_type=jnp.float32
    )
    grad_window = jnp.concatenate(
        [keys_gradient.reshape(span_rows, kv_cols), values_gradient.reshape(span_rows, kv_cols)], 1
    )
    grad_kv = grad_window[leading_part:]
    for steps in range(reach, 0, -1):
        start = (reach - steps) * TOK_DEV
        block = grad_window[start : start + TOK_DEV].astype(jnp.bfloat16)
        grad_kv = grad_kv + shifted(block, "tok", -steps).astype(jnp.float32)
    _, query_pull = jax.vjp(
        lambda raw_values: prepare_inputs(raw_values, query_norm_gain, cosine_table, sine_table),
        query_heads_raw,
    )
    _, key_pullback = jax.vjp(
        lambda raw_values: prepare_inputs(raw_values, key_gain, cosine_table, sine_table),
        key_heads_raw,
    )
    query_back = (
        query_pull(grad_queries.reshape(TOK_DEV, query_heads, HEAD_SIZE))[0]
        .astype(jnp.bfloat16)
        .reshape(TOK_DEV, query_cols)
    )
    query_sums = begin_scatter(full_rows, query_back, "tok")
    grad_kv, (query_sums,) = ordered(grad_kv, query_sums)
    key_backward = (
        key_pullback(grad_kv[:, :kv_cols].reshape(TOK_DEV, key_value_heads, HEAD_SIZE))[0]
        .astype(jnp.bfloat16)
        .reshape(TOK_DEV, kv_cols)
    )
    value_backward = grad_kv[:, kv_cols:].astype(jnp.bfloat16)
    kv_back = jnp.concatenate([key_backward, value_backward], 1)
    out_sums = begin_scatter(all_heads, grad_out, "tok")
    kv_back, (out_sums,) = ordered(kv_back, out_sums)
    query_near, query_far = exchange_far(query_sums, "tok")
    out_near, out_far = exchange_far(out_sums, "tok")
    kv_later, query_far = lax.optimization_barrier((kv_back, query_far))
    kv_last, out_far = lax.optimization_barrier((kv_back, out_far))
    block_rows = jnp.zeros((TOK_DEV, full_rows.shape[1]), jnp.bfloat16)
    for offset in range(len(query_pieces)):
        kv_used = kv_back if 2 * offset < len(query_pieces) else kv_later
        product = jnp.einsum(
            "tc,dc->td", query_back, query_pieces[offset], preferred_element_type=jnp.float32
        ) + jnp.einsum("tc,dc->td", kv_used, kv_pieces[offset], preferred_element_type=jnp.float32)
        start = (block_index ^ offset) * height
        block_rows = lax.dynamic_update_slice_in_dim(
            block_rows, product.astype(jnp.bfloat16), start, 1
        )
    grad_x = lax.psum_scatter(block_rows, "hid", scatter_dimension=1, tiled=True)
    kv_sums = begin_scatter(full_rows, kv_last, "tok")
    grad_wq = finish((query_near, query_far))
    grad_wo = finish((out_near, out_far))
    grad_wkv = finish(exchange_far(kv_sums, "tok"))
    key_weight_gradient = grad_wkv[:, :kv_cols]
    value_weight_gradient = grad_wkv[:, kv_cols:]
    return (attn_out, grad_x, grad_wq, key_weight_gradient, value_weight_gradient, grad_wo)


def solution(mesh):
    return jax.shard_map(
        local,
        mesh=mesh,
        in_specs=(
            P(("groups", "tok"), "hid"),
            P("tok", "hid"),
            P("tok", "hid"),
            P("tok", "hid"),
            P("tok", "hid"),
            P(),
            P(),
            P("groups"),
            P(("groups", "tok"), "hid"),
        ),
        out_specs=(
            P(("groups", "tok"), "hid"),
            P(("groups", "tok"), "hid"),
            P(("groups", "tok"), "hid"),
            P(("groups", "tok"), "hid"),
            P(("groups", "tok"), "hid"),
            P(("groups", "tok"), "hid"),
        ),
        check_vma=False,
    )
```

```python
import jax
import jax.numpy as jnp
from jax import lax
from jax.sharding import PartitionSpec as P

QUERY_HEADS = 16
KEY_VALUE_HEADS = 8
HEAD_SIZE = 128
WINDOW = 1024
TOK_DEV = 256


attn_scale = 168.0 ** (-0.5)
rope_base = 10000.0
norm_eps = 1e-06


def shifted(value, axis, steps):
    count = lax.axis_size(axis)
    first, last = (max(0, -steps), min(count, count - steps))
    return lax.ppermute(value, axis, [(source, source + steps) for source in range(first, last)])


def swapped(value, axis, bit):
    count = lax.axis_size(axis)
    return lax.ppermute(value, axis, [(source, source ^ bit) for source in range(count)])


def gather_swapped(value, axis):
    count = lax.axis_size(axis)
    held = {0: value}
    bit = count // 2
    while bit:
        for offset in list(held):
            held[offset ^ bit] = swapped(held[offset], axis, bit)
        bit //= 2
    return [held[offset] for offset in range(count)]


def begin_scatter(left, right, axis):
    count = lax.axis_size(axis)
    index = lax.axis_index(axis)
    height = left.shape[1] // count

    def product(offset):
        picked = lax.dynamic_slice_in_dim(left, (index ^ offset) * height, height, 1)
        return jnp.einsum("td,tc->dc", picked, right, preferred_element_type=jnp.float32)

    totals = {}
    for offset in range(count - 2, -1, -2):
        arrived = swapped(product(offset ^ 1).astype(jnp.bfloat16), axis, 1)
        totals[offset] = product(offset) + arrived.astype(jnp.float32)
        if offset:
            totals[offset] = totals[offset].astype(jnp.bfloat16)
    return totals


def exchange_far(totals, axis):
    count = lax.axis_size(axis)
    totals = dict(totals)
    bit = 2
    while bit < count:
        for offset in range(count - bit, 0, -2 * bit):
            arrived = swapped(totals[offset], axis, bit)
            kept = offset ^ bit
            if kept == 0 and 2 * bit == count:
                return totals[0], arrived
            total = totals[kept].astype(jnp.float32) + arrived.astype(jnp.float32)
            totals[kept] = total.astype(jnp.bfloat16) if kept else total
        bit *= 2
    return totals[0], jnp.zeros_like(totals[0], jnp.bfloat16)


def finish(pair):
    return pair[0] + pair[1].astype(jnp.float32)


def ordered(value, *groups):
    sent = [{key: total for key, total in group.items() if key} for group in groups]
    value, sent = lax.optimization_barrier((value, sent))
    return value, [{**group, **part} for group, part in zip(groups, sent)]


def rotary_tables(token_pos):
    half_dim = HEAD_SIZE // 2
    freqs = rope_base ** (-jnp.arange(half_dim, dtype=jnp.float32) * 2.0 / HEAD_SIZE)
    angles = token_pos.astype(jnp.float32)[:, None] * freqs[None, :]
    return (jnp.cos(angles), jnp.sin(angles))


def prepare_inputs(raw_values, gain_vector, cosine_table, sine_table):
    scaled = (
        raw_values
        * lax.rsqrt(jnp.mean(raw_values * raw_values, -1, keepdims=True) + norm_eps)
        * gain_vector
    )
    half_dim = scaled.shape[-1] // 2
    first_half = scaled[..., :half_dim]
    second_half = scaled[..., half_dim:]
    cos_rows = cosine_table[:, None, :]
    sin_rows = sine_table[:, None, :]
    return jnp.concatenate(
        [
            first_half * cos_rows - second_half * sin_rows,
            second_half * cos_rows + first_half * sin_rows,
        ],
        -1,
    )


def local(
    tokens, w_query, key_weight, value_weight, w_out, query_norm_gain, key_gain, positions, grad_out
):
    hidden_count = lax.axis_size("hid")
    block_index = lax.axis_index("tok")
    query_heads = QUERY_HEADS // hidden_count
    key_value_heads = KEY_VALUE_HEADS // hidden_count
    group_width = QUERY_HEADS // KEY_VALUE_HEADS
    reach = min(WINDOW // TOK_DEV, lax.axis_size("tok") - 1)
    span_rows = (reach + 1) * TOK_DEV
    leading_part = reach * TOK_DEV
    first_token = block_index * TOK_DEV
    query_cols = query_heads * HEAD_SIZE
    kv_cols = key_value_heads * HEAD_SIZE
    full_rows = lax.all_gather(tokens, "hid", axis=1, tiled=True)
    query_pieces = gather_swapped(w_query, "tok")
    kv_pieces = gather_swapped(jnp.concatenate([key_weight, value_weight], 1), "tok")
    full_wo = lax.all_gather(w_out, "tok", axis=0, tiled=True)
    height = w_query.shape[0]

    def project(pieces):
        total = 0.0
        for offset, piece in enumerate(pieces):
            start = (block_index ^ offset) * height
            columns = lax.dynamic_slice_in_dim(full_rows, start, height, 1)
            total = total + jnp.dot(columns, piece, preferred_element_type=jnp.float32)
        return total

    kv_unnormed = project(kv_pieces)
    query_unnormed = project(query_pieces)
    key_unnormed = kv_unnormed[:, :kv_cols]
    value_raw = kv_unnormed[:, kv_cols:]
    partial_heads = jnp.einsum("td,hd->th", grad_out, full_wo, preferred_element_type=jnp.float32)
    partial_heads = partial_heads.astype(jnp.bfloat16)
    attended_gradient = lax.psum_scatter(partial_heads, "hid", scatter_dimension=1, tiled=True)
    values_local = value_raw.astype(jnp.bfloat16)
    token_pos = lax.dynamic_slice_in_dim(positions, first_token, TOK_DEV, 0)
    cosine_table, sine_table = rotary_tables(token_pos)
    query_heads_raw = query_unnormed.reshape(TOK_DEV, query_heads, HEAD_SIZE)
    key_heads_raw = key_unnormed.reshape(TOK_DEV, key_value_heads, HEAD_SIZE)
    query_rows = (
        prepare_inputs(query_heads_raw, query_norm_gain, cosine_table, sine_table)
        .astype(jnp.bfloat16)
        .reshape(TOK_DEV, key_value_heads, group_width, HEAD_SIZE)
    )
    keys_local = prepare_inputs(key_heads_raw, key_gain, cosine_table, sine_table).astype(
        jnp.bfloat16
    )
    key_value = jnp.concatenate([keys_local.reshape(TOK_DEV, kv_cols), values_local], 1)
    blocks = [shifted(key_value, "tok", steps) for steps in range(reach, 0, -1)] + [key_value]
    window = jnp.concatenate(blocks, 0)
    key_window = window[:, :kv_cols].reshape(span_rows, key_value_heads, HEAD_SIZE)
    value_window = window[:, kv_cols:].reshape(span_rows, key_value_heads, HEAD_SIZE)
    query_index = first_token + jnp.arange(TOK_DEV, dtype=jnp.int32)
    key_index = first_token - leading_part + jnp.arange(span_rows, dtype=jnp.int32)
    padded_pos = jnp.pad(positions, (leading_part, 0))
    key_pos = lax.dynamic_slice_in_dim(padded_pos, first_token, span_rows, 0)
    distance = query_index[:, None] - key_index[None, :]
    allowed = (
        (key_index[None, :] >= 0)
        & (distance >= 0)
        & (distance < WINDOW)
        & (token_pos[:, None] - key_pos[None, :] == distance)
    )
    scores = (
        jnp.einsum("tkgd,ukd->kgtu", query_rows, key_window, preferred_element_type=jnp.float32)
        * attn_scale
    )
    weights = jnp.where(allowed[None, None], jnp.exp(scores), 0.0)
    probabilities = weights / jnp.sum(weights, -1, keepdims=True)
    rounded = probabilities.astype(jnp.bfloat16)
    attended = jnp.einsum(
        "kgtu,ukd->tkgd", rounded, value_window, preferred_element_type=jnp.float32
    )
    attended = attended.astype(jnp.bfloat16).reshape(TOK_DEV, query_cols)
    attended, attended_gradient = lax.optimization_barrier((attended, attended_gradient))
    all_heads = lax.all_gather(attended, "hid", axis=1, tiled=True)
    output = jnp.dot(all_heads, full_wo, preferred_element_type=jnp.float32)
    attn_out = output.astype(jnp.bfloat16)
    attended_gradient = attended_gradient.reshape(TOK_DEV, key_value_heads, group_width, HEAD_SIZE)
    grad_probs = jnp.einsum(
        "tkgd,ukd->kgtu", attended_gradient, value_window, preferred_element_type=jnp.float32
    )
    grad_scores = (
        attn_scale
        * probabilities
        * (grad_probs - jnp.sum(probabilities * grad_probs, -1, keepdims=True))
    )
    grad_scores = grad_scores.astype(jnp.bfloat16)
    grad_queries = jnp.einsum(
        "kgtu,ukd->tkgd", grad_scores, key_window, preferred_element_type=jnp.float32
    )
    keys_gradient = jnp.einsum(
        "kgtu,tkgd->ukd", grad_scores, query_rows, preferred_element_type=jnp.float32
    )
    values_gradient = jnp.einsum(
        "kgtu,tkgd->ukd", rounded, attended_gradient, preferred_element_type=jnp.float32
    )
    grad_window = jnp.concatenate(
        [keys_gradient.reshape(span_rows, kv_cols), values_gradient.reshape(span_rows, kv_cols)], 1
    )
    grad_kv = grad_window[leading_part:]
    for steps in range(reach, 0, -1):
        start = (reach - steps) * TOK_DEV
        block = grad_window[start : start + TOK_DEV].astype(jnp.bfloat16)
        grad_kv = grad_kv + shifted(block, "tok", -steps).astype(jnp.float32)
    _, query_pull = jax.vjp(
        lambda raw_values: prepare_inputs(raw_values, query_norm_gain, cosine_table, sine_table),
        query_heads_raw,
    )
    _, key_pullback = jax.vjp(
        lambda raw_values: prepare_inputs(raw_values, key_gain, cosine_table, sine_table),
        key_heads_raw,
    )
    query_back = (
        query_pull(grad_queries.reshape(TOK_DEV, query_heads, HEAD_SIZE))[0]
        .astype(jnp.bfloat16)
        .reshape(TOK_DEV, query_cols)
    )
    query_sums = begin_scatter(full_rows, query_back, "tok")
    grad_kv, (query_sums,) = ordered(grad_kv, query_sums)
    key_backward = (
        key_pullback(grad_kv[:, :kv_cols].reshape(TOK_DEV, key_value_heads, HEAD_SIZE))[0]
        .astype(jnp.bfloat16)
        .reshape(TOK_DEV, kv_cols)
    )
    value_backward = grad_kv[:, kv_cols:].astype(jnp.bfloat16)
    kv_back = jnp.concatenate([key_backward, value_backward], 1)
    out_sums = begin_scatter(all_heads, grad_out, "tok")
    kv_back, (out_sums,) = ordered(kv_back, out_sums)
    query_near, query_far = exchange_far(query_sums, "tok")
    out_near, out_far = exchange_far(out_sums, "tok")
    kv_last, out_far = lax.optimization_barrier((kv_back, out_far))
    block_rows = jnp.zeros((TOK_DEV, full_rows.shape[1]), jnp.bfloat16)
    for offset in range(len(query_pieces)):
        product = jnp.einsum(
            "tc,dc->td", query_back, query_pieces[offset], preferred_element_type=jnp.float32
        ) + jnp.einsum("tc,dc->td", kv_back, kv_pieces[offset], preferred_element_type=jnp.float32)
        start = (block_index ^ offset) * height
        block_rows = lax.dynamic_update_slice_in_dim(
            block_rows, product.astype(jnp.bfloat16), start, 1
        )
    block_rows, query_far = lax.optimization_barrier((block_rows, query_far))
    grad_x = lax.psum_scatter(block_rows, "hid", scatter_dimension=1, tiled=True)
    kv_sums = begin_scatter(full_rows, kv_last, "tok")
    grad_wq = finish((query_near, query_far))
    grad_wo = finish((out_near, out_far))
    grad_wkv = finish(exchange_far(kv_sums, "tok"))
    key_weight_gradient = grad_wkv[:, :kv_cols]
    value_weight_gradient = grad_wkv[:, kv_cols:]
    return (attn_out, grad_x, grad_wq, key_weight_gradient, value_weight_gradient, grad_wo)


def solution(mesh):
    return jax.shard_map(
        local,
        mesh=mesh,
        in_specs=(
            P(("groups", "tok"), "hid"),
            P("tok", "hid"),
            P("tok", "hid"),
            P("tok", "hid"),
            P("tok", "hid"),
            P(),
            P(),
            P("groups"),
            P(("groups", "tok"), "hid"),
        ),
        out_specs=(
            P(("groups", "tok"), "hid"),
            P(("groups", "tok"), "hid"),
            P(("groups", "tok"), "hid"),
            P(("groups", "tok"), "hid"),
            P(("groups", "tok"), "hid"),
            P(("groups", "tok"), "hid"),
        ),
        check_vma=False,
    )
```
